32 devices in a mesh: qrow: 8 (over y, x, core), kcol: 4 (over z).
Axes of the slice: x: 2, y: 2, z: 4, core: 2. Of those that a mesh axis runs over, the one named last changes fastest.
Arguments:
- queries: bfloat16 [4096, 1024], P(('qrow', 'kcol')), may hold values from -6 to 6
- keys: bfloat16 [4096, 128], P(('qrow', 'kcol')), may hold values from -6 to 6
- values: bfloat16 [4096, 128], P(('qrow', 'kcol')), may hold values from -6 to 6
- grad_out: bfloat16 [4096, 1024], P(('qrow', 'kcol')), may hold values from -96 to 96
- block_order: int32 [32], replicated, may hold values from 0 to 31, each once
Outputs:
- grad_queries: bfloat16 [4096, 1024], P(('qrow', 'kcol'))
- grad_keys: bfloat16 [4096, 128], P(('qrow', 'kcol'))
- grad_values: bfloat16 [4096, 128], P(('qrow', 'kcol'))
The draws below stay inside these ranges and needn't reach their ends.
Inputs may be any that keep to these rules, and one draw needn't show every extreme that they name: `block_order`: each of the 32 block numbers appears once.
All inputs are finite; a program needn't handle non-finite values.
Results may differ from the reference program's by a relative error of at most 0.0076.
Values may be sent and summed in bfloat16 or wider, within the bound.
A program may use at most 128 MiB of HBM per device.

```python
import math
import jax
import jax.numpy as jnp
from jax import lax

H = 8
HD = 128
TOK_DEV = 128
BLOCKS = 32
SEQ = 4096


def draw_queries(key, part):
    key = jax.random.fold_in(key, 11)
    result = jnp.clip(jax.random.normal(key, (SEQ, H * HD), dtype=jnp.float32), -6.0, 6.0)
    return result.astype(jnp.bfloat16)


def draw_keys(key, part):
    key = jax.random.fold_in(key, 23)
    result = jnp.clip(jax.random.normal(key, (SEQ, HD), dtype=jnp.float32), -6.0, 6.0)
    return result.astype(jnp.bfloat16)


def levels(stream_key, extent, shards, smallest, top_value):
    gain, own = 1.0, jax.random.fold_in(stream_key, 6)
    for position, shards_of in shards:
        steps = jnp.exp(jax.random.uniform(jax.random.fold_in(own, position), (shards_of,), jnp.float32, smallest / len(shards), top_value / len(shards)))
        gain = gain * jnp.repeat(steps, extent[position] // shards_of).reshape([-1 if axis == position else 1 for axis in range(len(extent))])
    return gain


def scatter_about(own_key, extent, spread, limit, cuts=(), kind=jnp.bfloat16):
    drawn = jax.random.normal(own_key, extent, jnp.float32) * spread
    if len(cuts) > 0:
        drawn = levels(own_key, extent, cuts, -0.22, 0.18) * drawn
    return jnp.clip(drawn, min=-limit, max=limit).astype(kind)


def setup_inputs(seed: int = 0) -> dict:
    arg_keys = jax.random.split(jax.random.key(seed), 6)
    queries = draw_queries(jax.random.fold_in(arg_keys[5], 71), 0)
    keys = draw_keys(jax.random.fold_in(arg_keys[5], 71), 0)
    values = scatter_about(arg_keys[2], (SEQ, HD), 1.0, 6.0, ((0, 32),))
    grad_out = scatter_about(arg_keys[3], (SEQ, H * HD), 16.0, 96.0, ((0, 32),))
    block_order = jax.random.permutation(arg_keys[4], BLOCKS).astype(jnp.int32)
    return dict(queries=queries, keys=keys, values=values, grad_out=grad_out, block_order=block_order)


NEG = -1e+30

def positions(block_order):
    offsets = jnp.arange(TOK_DEV, dtype=jnp.int32)
    return (block_order.astype(jnp.int32)[:, None] * TOK_DEV + offsets[None, :]).reshape(-1).astype(jnp.int32)

def reference(queries, keys, values, grad_out, block_order):
    inverse_root = 1.0 / math.sqrt(HD)
    place = positions(block_order)
    width = min(512, SEQ)
    count = SEQ // width
    key_wide = keys.astype(jnp.float32)
    value_wide = values.astype(jnp.float32)
    query_blocks = queries.reshape(count, width, H, HD)
    grad_blocks = grad_out.reshape(count, width, H, HD)
    place_blocks = place.reshape(count, width)

    def step(carry, items):
        key_sum, value_sum = carry
        query_part, grad_part, query_place = items
        query_wide = query_part.astype(jnp.float32)
        grad_wide = grad_part.astype(jnp.float32)
        scores = jnp.einsum('qhd,kd->hqk', query_wide, key_wide) * inverse_root
        visible = place[None, None, :] <= query_place[None, :, None]
        masked = jnp.where(visible, scores, NEG)
        top = lax.optimization_barrier(jnp.max(masked, axis=2, keepdims=True))
        raised = jnp.where(visible, jnp.exp(masked - top), 0.0)
        total = lax.optimization_barrier(jnp.sum(raised, axis=2, keepdims=True))
        attention = raised / total
        grad_weights = jnp.einsum('qhd,kd->hqk', grad_wide, value_wide)
        delta = lax.optimization_barrier(jnp.sum(attention * grad_weights, axis=2, keepdims=True))
        attention_low = attention.astype(jnp.bfloat16)
        grad_scores = (attention * (grad_weights - delta)).astype(jnp.bfloat16)
        value_sum = value_sum + jnp.einsum('hqk,qhd->kd', attention_low.astype(jnp.float32), grad_wide)
        key_sum = key_sum + jnp.einsum('hqk,qhd->kd', grad_scores.astype(jnp.float32), query_wide) * inverse_root
        grad_query = jnp.einsum('hqk,kd->qhd', grad_scores.astype(jnp.float32), key_wide) * inverse_root
        return ((key_sum, value_sum), grad_query.astype(jnp.bfloat16))
    start = (jnp.zeros((SEQ, HD), jnp.float32), jnp.zeros((SEQ, HD), jnp.float32))
    (key_sum, value_sum), grad_queries = lax.scan(step, start, (query_blocks, grad_blocks, place_blocks))
    return (grad_queries.reshape(SEQ, H * HD), key_sum.astype(jnp.bfloat16), value_sum.astype(jnp.bfloat16))
```

```python
import functools
import math

import jax
import jax.numpy as jnp
from jax import lax
from jax.experimental import pallas as pl
from jax.experimental.pallas import tpu as pltpu
from jax.sharding import PartitionSpec as P

HD = 128
BIG = 1e30
F32 = jnp.float32
BF16 = jnp.bfloat16
ROOT = 1.0 / math.sqrt(HD)
SCALE = ROOT / math.log(2.0)
MESH = pl.DeviceIdType.MESH


def nn(a, b):
    return lax.dot_general(a, b, (((1,), (0,)), ((), ())), preferred_element_type=F32)


def nt(a, b):
    return lax.dot_general(a, b, (((1,), (1,)), ((), ())), preferred_element_type=F32)


def tn(a, b):
    return lax.dot_general(a, b, (((0,), (0,)), ((), ())), preferred_element_type=F32)


def kernel(
    rows_count, cols_count, length, heads, tile,
    order, q_ref, k_ref, v_ref, g_ref, dq_ref, dk_ref, dv_ref,
    kv, raised, qt, gt, tops, top, total, out_t, delta, dq_t, diag,
    own_sum, chip_sum, peer_send, peer_recv, chip_recv, col_recv,
    s1, r1, s2, r2, s3, r3, s4, r4, s5, r5, s6, r6,
):
    chips = rows_count // 2
    row = lax.axis_index("qrow")
    col = lax.axis_index("kcol")
    chip = lax.div(row, 2)
    core = lax.rem(row, 2)
    peer = chip * 2 + (1 - core)
    me = row * cols_count + col
    span = cols_count * length
    subs = span // tile
    lanes = heads * length

    def other_col(k):
        return (row, lax.rem(col + k, cols_count))

    def other_chip(k):
        return (lax.rem(chip + k, chips) * 2 + core, col)

    def source_row(k, which):
        return lax.rem(chip + chips - k, chips) * 2 + which

    def target_row(k, which):
        return lax.rem(chip + k, chips) * 2 + which

    barrier = pltpu.get_barrier_semaphore()
    for k in range(1, cols_count):
        pl.semaphore_signal(barrier, inc=1, device_id=other_col(k), device_id_type=MESH)
    for k in range(1, chips):
        pl.semaphore_signal(barrier, inc=1, device_id=other_chip(k), device_id_type=MESH)
    pl.semaphore_signal(barrier, inc=1, device_id=(peer, col), device_id_type=MESH)
    own = pl.ds(pl.multiple_of(col * length, length), length)
    kv[row, own, 0:HD] = k_ref[...]
    kv[row, own, HD : 2 * HD] = v_ref[...]
    pl.semaphore_wait(barrier, cols_count + chips - 1)

    def copy_col(k):
        part = kv.at[row, own]
        return pltpu.make_async_remote_copy(
            src_ref=part, dst_ref=part, send_sem=s1.at[k], recv_sem=r1.at[k],
            device_id=other_col(k), device_id_type=MESH,
        )

    def copy_chip(k):
        return pltpu.make_async_remote_copy(
            src_ref=kv.at[row], dst_ref=kv.at[row], send_sem=s2.at[k], recv_sem=r2.at[k],
            device_id=other_chip(k), device_id_type=MESH,
        )

    def copy_core(k):
        part = kv.at[source_row(k, core)]
        return pltpu.make_async_remote_copy(
            src_ref=part, dst_ref=part, send_sem=s3.at[k], recv_sem=r3.at[k],
            device_id=(peer, col), device_id_type=MESH,
        )

    for k in range(1, cols_count):
        copy_col(k).start()

    for h in range(heads):
        cut = slice(h * HD, (h + 1) * HD)
        put = slice(h * length, (h + 1) * length)
        qt[:, put] = q_ref[:, cut].T
        gt[:, put] = g_ref[:, cut].T

    key_at = lax.broadcasted_iota(jnp.int32, (length, lanes), 0)
    row_at = lax.rem(lax.broadcasted_iota(jnp.int32, (length, lanes), 1), length)
    scores = jnp.where(key_at <= row_at, nn(k_ref[...], qt[...]), -BIG)
    first = jnp.max(scores, axis=0, keepdims=True)
    own_raised = jnp.exp2((scores - first) * SCALE)
    own_low = own_raised.astype(BF16)
    diag[...] = own_low
    top[...] = first
    tops[rows_count * subs] = first
    total[...] = jnp.sum(own_raised, axis=0, keepdims=True)
    out_t[...] = tn(v_ref[...], own_low)

    def hidden(block):
        return jnp.where(order[block] < order[me], 0.0, BIG).astype(F32)

    def forward(which):
        @pl.loop(0, subs)
        def _(sub):
            at = pl.ds(pl.multiple_of(sub * tile, tile), tile)
            scores = nn(kv[which, at, 0:HD], qt[...])
            first_block = which * cols_count + sub * (tile // length)
            old = top[...]
            new = old
            offs = []
            for b in range(tile // length):
                off = hidden(first_block + b)
                offs.append(off)
                part = scores[b * length : (b + 1) * length]
                new = jnp.maximum(new, jnp.max(part, axis=0, keepdims=True) - off)
            alpha = jnp.exp2((old - new) * SCALE)
            shift = new * SCALE
            parts = []
            add = jnp.zeros_like(old)
            for b in range(tile // length):
                part = scores[b * length : (b + 1) * length]
                up = jnp.exp2(part * SCALE - (shift + offs[b]))
                add = add + jnp.sum(up, axis=0, keepdims=True)
                parts.append(up.astype(BF16))
            low = jnp.concatenate(parts, axis=0)
            index = which * subs + sub
            raised[index] = low
            top[...] = new
            tops[index] = new
            total[...] = total[...] * alpha + add
            out_t[...] = out_t[...] * alpha + tn(kv[which, at, HD : 2 * HD], low)

    for k in range(1, cols_count):
        copy_col(k).wait_recv()
    for k in range(1, chips):
        copy_chip(k).start()

    @pl.loop(0, chips)
    def _(k):
        @pl.when(k > 0)
        def _():
            copy_chip(k).wait_recv()

        copy_core(k).start()
        forward(source_row(k, core))
        copy_core(k).wait_recv()
        forward(source_row(k, 1 - core))

    inverse = 1.0 / total[...]
    delta[...] = (
        jnp.sum(out_t[...] * gt[...].astype(F32), axis=0, keepdims=True) * inverse
    )

    def terms(values, keys, low, index):
        grad_weights = nn(values, gt[...])
        grad_low = (grad_weights - delta[...]).astype(BF16) * low
        share = jnp.exp2((tops[index] - top[...]) * SCALE) / total[...]
        scaled_q = (qt[...].astype(F32) * (share * ROOT)).astype(BF16)
        scaled_g = (gt[...].astype(F32) * share).astype(BF16)
        grad_q = tn(keys, grad_low) * (share * ROOT)
        return nt(grad_low, scaled_q), nt(low, scaled_g), grad_q

    own_dk, own_dv, own_dq = terms(v_ref[...], k_ref[...], diag[...], rows_count * subs)
    own_sum[:, 0:HD] = own_dk
    own_sum[:, HD : 2 * HD] = own_dv
    dq_t[...] = own_dq

    def backward(which, store):
        @pl.loop(0, subs)
        def _(sub):
            at = pl.ds(pl.multiple_of(sub * tile, tile), tile)
            index = which * subs + sub
            grad_k, grad_v, grad_q = terms(
                kv[which, at, HD : 2 * HD], kv[which, at, 0:HD], raised[index], index
            )
            dq_t[...] += grad_q
            store(at, grad_k, grad_v)

    def give_core(k):
        return pltpu.make_async_remote_copy(
            src_ref=peer_send.at[k], dst_ref=peer_recv.at[k],
            send_sem=s4.at[k], recv_sem=r4.at[k],
            device_id=(peer, col), device_id_type=MESH,
        )

    def give_chip(k):
        return pltpu.make_async_remote_copy(
            src_ref=peer_recv.at[k], dst_ref=chip_recv.at[k],
            send_sem=s5.at[k], recv_sem=r5.at[k],
            device_id=other_chip(k), device_id_type=MESH,
        )

    def give_col(k):
        return pltpu.make_async_remote_copy(
            src_ref=peer_recv.at[0, pl.ds(lax.rem(col + k, cols_count) * length, length)],
            dst_ref=col_recv.at[k],
            send_sem=s6.at[k], recv_sem=r6.at[k],
            device_id=other_col(k), device_id_type=MESH,
        )

    @pl.loop(0, chips)
    def _(step):
        k = lax.rem(step + 1, chips)

        def to_peer(at, grad_k, grad_v):
            peer_send[k, at, 0:HD] = grad_k.astype(BF16)
            peer_send[k, at, HD : 2 * HD] = grad_v.astype(BF16)

        backward(target_row(k, 1 - core), to_peer)
        give_core(k).start()

        def to_sum(at, grad_k, grad_v):
            chip_sum[at, 0:HD] = grad_k
            chip_sum[at, HD : 2 * HD] = grad_v

        backward(target_row(k, core), to_sum)
        give_core(k).wait_recv()
        chip_sum[...] += peer_recv[k].astype(F32)

        @pl.when(k > 0)
        def _():
            peer_recv[k] = chip_sum[...].astype(BF16)
            give_chip(k).start()

    for k in range(1, chips):
        give_chip(k).wait_recv()
        chip_sum[...] += chip_recv[k].astype(F32)
    peer_recv[0] = chip_sum[...].astype(BF16)
    for k in range(1, cols_count):
        give_col(k).start()
    for h in range(heads):
        cut = slice(h * HD, (h + 1) * HD)
        put = slice(h * length, (h + 1) * length)
        dq_ref[:, cut] = dq_t[:, put].T.astype(BF16)
    last = chip_sum[own] + own_sum[...]
    for k in range(1, cols_count):
        give_col(k).wait_recv()
        last = last + col_recv[k].astype(F32)
    dk_ref[...] = last[:, 0:HD].astype(BF16)
    dv_ref[...] = last[:, HD : 2 * HD].astype(BF16)

    for k in range(1, cols_count):
        copy_col(k).wait_send()
        give_col(k).wait_send()
    for k in range(1, chips):
        copy_chip(k).wait_send()
        give_chip(k).wait_send()
    for k in range(chips):
        copy_core(k).wait_send()
        give_core(k).wait_send()


def per_device(queries, keys, values, grad_out, block_order):
    rows_count = lax.axis_size("qrow")
    cols_count = lax.axis_size("kcol")
    length = queries.shape[0]
    heads = queries.shape[1] // HD
    chips = rows_count // 2
    span = cols_count * length
    tile = min(512, span)
    subs = span // tile
    lanes = heads * length
    vmem = pl.BlockSpec(memory_space=pltpu.VMEM)
    dma = pltpu.SemaphoreType.DMA
    return pl.pallas_call(
        functools.partial(kernel, rows_count, cols_count, length, heads, tile),
        out_shape=(
            jax.ShapeDtypeStruct(queries.shape, BF16),
            jax.ShapeDtypeStruct(keys.shape, BF16),
            jax.ShapeDtypeStruct(values.shape, BF16),
        ),
        in_specs=[pl.BlockSpec(memory_space=pltpu.SMEM)] + [vmem] * 4,
        out_specs=(vmem, vmem, vmem),
        scratch_shapes=[
            pltpu.VMEM((rows_count, span, 2 * HD), BF16),
            pltpu.VMEM((rows_count * subs, tile, lanes), BF16),
            pltpu.VMEM((HD, lanes), BF16),
            pltpu.VMEM((HD, lanes), BF16),
            pltpu.VMEM((rows_count * subs + 1, 1, lanes), F32),
            pltpu.VMEM((1, lanes), F32),
            pltpu.VMEM((1, lanes), F32),
            pltpu.VMEM((HD, lanes), F32),
            pltpu.VMEM((1, lanes), F32),
            pltpu.VMEM((HD, lanes), F32),
            pltpu.VMEM((length, lanes), BF16),
            pltpu.VMEM((length, 2 * HD), F32),
            pltpu.VMEM((span, 2 * HD), F32),
            pltpu.VMEM((chips, span, 2 * HD), BF16),
            pltpu.VMEM((chips, span, 2 * HD), BF16),
            pltpu.VMEM((chips, span, 2 * HD), BF16),
            pltpu.VMEM((cols_count, length, 2 * HD), BF16),
            dma((cols_count,)), dma((cols_count,)),
            dma((chips,)), dma((chips,)),
            dma((chips,)), dma((chips,)),
            dma((chips,)), dma((chips,)),
            dma((chips,)), dma((chips,)),
            dma((cols_count,)), dma((cols_count,)),
        ],
        compiler_params=pltpu.CompilerParams(
            collective_id=0, has_side_effects=True, vmem_limit_bytes=62 * 1024 * 1024
        ),
    )(block_order, queries, keys, values, grad_out)


def solution(mesh):
    return jax.shard_map(
        per_device,
        mesh=mesh,
        in_specs=(
            P(("qrow", "kcol"), None),
            P(("qrow", "kcol"), None),
            P(("qrow", "kcol"), None),
            P(("qrow", "kcol"), None),
            P(),
        ),
        out_specs=(P(("qrow", "kcol"), None), P(("qrow", "kcol"), None), P(("qrow", "kcol"), None)),
        check_vma=False,
    )
```

```python
import functools
import math

import jax
import jax.numpy as jnp
from jax import lax
from jax.experimental import pallas as pl
from jax.experimental.pallas import tpu as pltpu
from jax.sharding import PartitionSpec as P

HD = 128
BIG = 1e30
F32 = jnp.float32
BF16 = jnp.bfloat16
ROOT = 1.0 / math.sqrt(HD)
SCALE = ROOT / math.log(2.0)
MESH = pl.DeviceIdType.MESH


def nn(a, b):
    return lax.dot_general(a, b, (((1,), (0,)), ((), ())), preferred_element_type=F32)


def nt(a, b):
    return lax.dot_general(a, b, (((1,), (1,)), ((), ())), preferred_element_type=F32)


def tn(a, b):
    return lax.dot_general(a, b, (((0,), (0,)), ((), ())), preferred_element_type=F32)


def kernel(
    rows_count, cols_count, length, heads, tile,
    order, q_ref, k_ref, v_ref, g_ref, dq_ref, dk_ref, dv_ref,
    kv, raised, qt, gt, tops, top, total, out_t, delta, dq_t, diag,
    own_sum, chip_sum, keep, peer_send, peer_recv, chip_recv, col_send, col_recv,
    s1, r1, s2, r2, s3, r3, s4, r4, s5, r5, s6, r6,
):
    chips = rows_count // 2
    row = lax.axis_index("qrow")
    col = lax.axis_index("kcol")
    chip = lax.div(row, 2)
    core = lax.rem(row, 2)
    far = 1 - core
    peer = chip * 2 + far
    me = row * cols_count + col
    span = chips * length
    subs = span // tile
    lanes = heads * length

    def later_col(k):
        return lax.rem(col + k, cols_count)

    def earlier_col(k):
        return lax.rem(col + cols_count - k, cols_count)

    def later_chip(c):
        return lax.rem(chip + c, chips)

    def earlier_chip(c):
        return lax.rem(chip + chips - c, chips)

    def piece(c):
        return pl.ds(pl.multiple_of(c * length, length), length)

    barrier = pltpu.get_barrier_semaphore()
    partners = [(row, later_col(k)) for k in range(1, cols_count)]
    partners += [(later_chip(c) * 2 + core, col) for c in range(1, chips)]
    partners += [(peer, col)]
    for partner in partners:
        pl.semaphore_signal(barrier, inc=1, device_id=partner, device_id_type=MESH)
    own = piece(chip)
    kv[col, core, own, 0:HD] = k_ref[...]
    kv[col, core, own, HD : 2 * HD] = v_ref[...]

    for h in range(heads):
        cut = slice(h * HD, (h + 1) * HD)
        put = slice(h * length, (h + 1) * length)
        qt[:, put] = q_ref[:, cut].T
        gt[:, put] = g_ref[:, cut].T

    pl.semaphore_wait(barrier, len(partners))

    def copy_col(k):
        part = kv.at[col, core, own]
        return pltpu.make_async_remote_copy(
            src_ref=part, dst_ref=part, send_sem=s1.at[k], recv_sem=r1.at[k],
            device_id=(row, later_col(k)), device_id_type=MESH,
        )

    def copy_chip(k, c):
        part = kv.at[earlier_col(k), core, own]
        return pltpu.make_async_remote_copy(
            src_ref=part, dst_ref=part, send_sem=s2.at[k, c], recv_sem=r2.at[k, c],
            device_id=(later_chip(c) * 2 + core, col), device_id_type=MESH,
        )

    def copy_core(k, c):
        part = kv.at[earlier_col(k), core, piece(earlier_chip(c))]
        return pltpu.make_async_remote_copy(
            src_ref=part, dst_ref=part, send_sem=s3.at[k, c], recv_sem=r3.at[k, c],
            device_id=(peer, col), device_id_type=MESH,
        )

    def spread(k):
        for c in range(1, chips):
            copy_chip(k, c).start()
        copy_core(k, 0).start()

    for k in range(1, cols_count):
        copy_col(k).start()
    spread(0)

    key_at = lax.broadcasted_iota(jnp.int32, (length, lanes), 0)
    row_at = lax.rem(lax.broadcasted_iota(jnp.int32, (length, lanes), 1), length)
    scores = jnp.where(key_at <= row_at, nn(k_ref[...], qt[...]), -BIG)
    first = jnp.max(scores, axis=0, keepdims=True)
    own_raised = jnp.exp2((scores - first) * SCALE)
    own_low = own_raised.astype(BF16)
    diag[...] = own_low
    top[...] = first
    tops[2 * cols_count * subs] = first
    total[...] = jnp.sum(own_raised, axis=0, keepdims=True)
    out_t[...] = tn(v_ref[...], own_low)

    def forward(key_col, which):
        @pl.loop(0, subs)
        def _(sub):
            at = pl.ds(pl.multiple_of(sub * tile, tile), tile)
            scores = nn(kv[key_col, which, at, 0:HD], qt[...])
            old = top[...]
            new = old
            offs = []
            for b in range(tile // length):
                block = ((sub * (tile // length) + b) * 2 + which) * cols_count + key_col
                off = jnp.where(order[block] < order[me], 0.0, BIG).astype(F32)
                offs.append(off)
                part = scores[b * length : (b + 1) * length]
                new = jnp.maximum(new, jnp.max(part, axis=0, keepdims=True) - off)
            alpha = jnp.exp2((old - new) * SCALE)
            shift = new * SCALE
            parts = []
            add = jnp.zeros_like(old)
            for b in range(tile // length):
                part = scores[b * length : (b + 1) * length]
                up = jnp.exp2(part * SCALE - (shift + offs[b]))
                add = add + jnp.sum(up, axis=0, keepdims=True)
                parts.append(up.astype(BF16))
            low = jnp.concatenate(parts, axis=0)
            index = (key_col * 2 + which) * subs + sub
            raised[index] = low
            top[...] = new
            tops[index] = new
            total[...] = total[...] * alpha + add
            out_t[...] = out_t[...] * alpha + tn(kv[key_col, which, at, HD : 2 * HD], low)

    @pl.loop(0, cols_count)
    def _(k):
        @pl.when(k < cols_count - 1)
        def _():
            copy_col(k + 1).wait_recv()
            spread(k + 1)

        for c in range(1, chips):
            copy_chip(k, c).wait_recv()
            copy_core(k, c).start()
        forward(earlier_col(k), core)
        for c in range(chips):
            copy_core(k, c).wait_recv()
        forward(earlier_col(k), far)

    inverse = 1.0 / total[...]
    delta[...] = (
        jnp.sum(out_t[...] * gt[...].astype(F32), axis=0, keepdims=True) * inverse
    )

    def terms(values, keys, low, index):
        grad_weights = nn(values, gt[...])
        grad_low = (grad_weights - delta[...]).astype(BF16) * low
        share = jnp.exp2((tops[index] - top[...]) * SCALE) / total[...]
        scaled_q = (qt[...].astype(F32) * (share * ROOT)).astype(BF16)
        scaled_g = (gt[...].astype(F32) * share).astype(BF16)
        grad_q = tn(keys, grad_low) * (share * ROOT)
        return nt(grad_low, scaled_q), nt(low, scaled_g), grad_q

    dq_t[...] = jnp.zeros_like(dq_t)

    def backward(key_col, which, store):
        @pl.loop(0, subs)
        def _(sub):
            at = pl.ds(pl.multiple_of(sub * tile, tile), tile)
            index = (key_col * 2 + which) * subs + sub
            grad_k, grad_v, grad_q = terms(
                kv[key_col, which, at, HD : 2 * HD],
                kv[key_col, which, at, 0:HD],
                raised[index],
                index,
            )
            dq_t[...] += grad_q
            store(at, grad_k, grad_v)

    def give_core(k):
        return pltpu.make_async_remote_copy(
            src_ref=peer_send.at[k], dst_ref=peer_recv.at[k],
            send_sem=s4.at[k], recv_sem=r4.at[k],
            device_id=(peer, col), device_id_type=MESH,
        )

    def give_chip(k, c):
        return pltpu.make_async_remote_copy(
            src_ref=peer_recv.at[k, piece(later_chip(c))], dst_ref=chip_recv.at[k, c],
            send_sem=s5.at[k, c], recv_sem=r5.at[k, c],
            device_id=(later_chip(c) * 2 + core, col), device_id_type=MESH,
        )

    def give_col(k):
        return pltpu.make_async_remote_copy(
            src_ref=col_send.at[k], dst_ref=col_recv.at[k],
            send_sem=s6.at[k], recv_sem=r6.at[k],
            device_id=(row, later_col(k)), device_id_type=MESH,
        )

    def column_sum(k):
        result = keep[k]
        for c in range(1, chips):
            give_chip(k, c).wait_recv()
            result = result + chip_recv[k, c].astype(F32)
        return result

    def pass_on(k):
        col_send[k] = column_sum(k).astype(BF16)
        give_col(k).start()

    @pl.loop(0, cols_count)
    def _(step):
        k = lax.rem(step + 1, cols_count)

        def to_peer(at, grad_k, grad_v):
            peer_send[k, at, 0:HD] = grad_k.astype(BF16)
            peer_send[k, at, HD : 2 * HD] = grad_v.astype(BF16)

        backward(later_col(k), far, to_peer)
        give_core(k).start()

        def to_sum(at, grad_k, grad_v):
            chip_sum[at, 0:HD] = grad_k
            chip_sum[at, HD : 2 * HD] = grad_v

        backward(later_col(k), core, to_sum)
        give_core(k).wait_recv()
        keep[k] = chip_sum[own] + peer_recv[k, own].astype(F32)
        peer_recv[k] = (chip_sum[...] + peer_recv[k].astype(F32)).astype(BF16)
        for c in range(1, chips):
            give_chip(k, c).start()

        @pl.when(step > 1)
        def _():
            pass_on(step - 1)

    own_dk, own_dv, own_dq = terms(
        v_ref[...], k_ref[...], diag[...], 2 * cols_count * subs
    )
    own_sum[:, 0:HD] = own_dk
    own_sum[:, HD : 2 * HD] = own_dv
    dq_t[...] += own_dq
    for k in range(max(1, cols_count - 1), cols_count):
        pass_on(k)
    for h in range(heads):
        cut = slice(h * HD, (h + 1) * HD)
        put = slice(h * length, (h + 1) * length)
        dq_ref[:, cut] = dq_t[:, put].T.astype(BF16)
    last = own_sum[...] + column_sum(0)
    for k in range(1, cols_count):
        give_col(k).wait_recv()
        last = last + col_recv[k].astype(F32)
    dk_ref[...] = last[:, 0:HD].astype(BF16)
    dv_ref[...] = last[:, HD : 2 * HD].astype(BF16)

    for k in range(1, cols_count):
        copy_col(k).wait_send()
        give_col(k).wait_send()
    for k in range(cols_count):
        give_core(k).wait_send()
        copy_core(k, 0).wait_send()
        for c in range(1, chips):
            copy_chip(k, c).wait_send()
            copy_core(k, c).wait_send()
            give_chip(k, c).wait_send()


def per_device(queries, keys, values, grad_out, block_order):
    rows_count = lax.axis_size("qrow")
    cols_count = lax.axis_size("kcol")
    length = queries.shape[0]
    heads = queries.shape[1] // HD
    chips = rows_count // 2
    span = chips * length
    tile = min(512, span)
    subs = span // tile
    lanes = heads * length
    vmem = pl.BlockSpec(memory_space=pltpu.VMEM)
    dma = pltpu.SemaphoreType.DMA
    return pl.pallas_call(
        functools.partial(kernel, rows_count, cols_count, length, heads, tile),
        out_shape=(
            jax.ShapeDtypeStruct(queries.shape, BF16),
            jax.ShapeDtypeStruct(keys.shape, BF16),
            jax.ShapeDtypeStruct(values.shape, BF16),
        ),
        in_specs=[pl.BlockSpec(memory_space=pltpu.SMEM)] + [vmem] * 4,
        out_specs=(vmem, vmem, vmem),
        scratch_shapes=[
            pltpu.VMEM((cols_count, 2, span, 2 * HD), BF16),
            pltpu.VMEM((2 * cols_count * subs, tile, lanes), BF16),
            pltpu.VMEM((HD, lanes), BF16),
            pltpu.VMEM((HD, lanes), BF16),
            pltpu.VMEM((2 * cols_count * subs + 1, 1, lanes), F32),
            pltpu.VMEM((1, lanes), F32),
            pltpu.VMEM((1, lanes), F32),
            pltpu.VMEM((HD, lanes), F32),
            pltpu.VMEM((1, lanes), F32),
            pltpu.VMEM((HD, lanes), F32),
            pltpu.VMEM((length, lanes), BF16),
            pltpu.VMEM((length, 2 * HD), F32),
            pltpu.VMEM((span, 2 * HD), F32),
            pltpu.VMEM((cols_count, length, 2 * HD), F32),
            pltpu.VMEM((cols_count, span, 2 * HD), BF16),
            pltpu.VMEM((cols_count, span, 2 * HD), BF16),
            pltpu.VMEM((cols_count, chips, length, 2 * HD), BF16),
            pltpu.VMEM((cols_count, length, 2 * HD), BF16),
            pltpu.VMEM((cols_count, length, 2 * HD), BF16),
            dma((cols_count,)), dma((cols_count,)),
            dma((cols_count, chips)), dma((cols_count, chips)),
            dma((cols_count, chips)), dma((cols_count, chips)),
            dma((cols_count,)), dma((cols_count,)),
            dma((cols_count, chips)), dma((cols_count, chips)),
            dma((cols_count,)), dma((cols_count,)),
        ],
        compiler_params=pltpu.CompilerParams(
            collective_id=0, has_side_effects=True, vmem_limit_bytes=62 * 1024 * 1024
        ),
    )(block_order, queries, keys, values, grad_out)


def solution(mesh):
    return jax.shard_map(
        per_device,
        mesh=mesh,
        in_specs=(
            P(("qrow", "kcol"), None),
            P(("qrow", "kcol"), None),
            P(("qrow", "kcol"), None),
            P(("qrow", "kcol"), None),
            P(),
        ),
        out_specs=(P(("qrow", "kcol"), None), P(("qrow", "kcol"), None), P(("qrow", "kcol"), None)),
        check_vma=False,
    )
```

```python
import functools
import math

import jax
import jax.numpy as jnp
from jax import lax
from jax.experimental import pallas as pl
from jax.experimental.pallas import tpu as pltpu
from jax.sharding import PartitionSpec as P

HD = 128
BIG = 1e30
F32 = jnp.float32
BF16 = jnp.bfloat16
ROOT = 1.0 / math.sqrt(HD)
SCALE = ROOT / math.log(2.0)
MESH = pl.DeviceIdType.MESH


def nn(a, b):
    return lax.dot_general(a, b, (((1,), (0,)), ((), ())), preferred_element_type=F32)


def nt(a, b):
    return lax.dot_general(a, b, (((1,), (1,)), ((), ())), preferred_element_type=F32)


def tn(a, b):
    return lax.dot_general(a, b, (((0,), (0,)), ((), ())), preferred_element_type=F32)


def kernel(
    rows_count, cols_count, length, heads, tile,
    order, q_ref, k_ref, v_ref, g_ref, dq_ref, dk_ref, dv_ref,
    kv, raised, qt, gt, tops, top, total, out_t, delta, dq_t, diag,
    own_sum, chip_sum, keep, peer_send, peer_recv, chip_recv, col_send, col_recv,
    s1, r1, s2, r2, s3, r3, s4, r4, s5, r5, s6, r6,
):
    chips = rows_count // 2
    row = lax.axis_index("qrow")
    col = lax.axis_index("kcol")
    chip = lax.div(row, 2)
    core = lax.rem(row, 2)
    far = 1 - core
    peer = chip * 2 + far
    me = row * cols_count + col
    span = chips * length
    subs = span // tile
    lanes = heads * length

    def later_col(k):
        return lax.rem(col + k, cols_count)

    def earlier_col(k):
        return lax.rem(col + cols_count - k, cols_count)

    square = chips == 4
    far_x = chip + 1 - 2 * lax.rem(chip, 2)
    far_y = chip + 2 - 4 * lax.div(chip, 2)

    def later_chip(c):
        if square:
            return (chip, far_x, far_y, 3 - chip)[c]
        return lax.rem(chip + c, chips)

    def earlier_chip(c):
        if square:
            return (chip, far_x, far_y, 3 - chip)[c]
        return lax.rem(chip + chips - c, chips)

    def piece(c):
        return pl.ds(pl.multiple_of(c * length, length), length)

    barrier = pltpu.get_barrier_semaphore()
    partners = [(row, later_col(k)) for k in range(1, cols_count)]
    partners += [(later_chip(c) * 2 + core, col) for c in range(1, chips)]
    partners += [(peer, col)]
    for partner in partners:
        pl.semaphore_signal(barrier, inc=1, device_id=partner, device_id_type=MESH)
    own = piece(chip)
    kv[col, core, own, 0:HD] = k_ref[...]
    kv[col, core, own, HD : 2 * HD] = v_ref[...]

    for h in range(heads):
        cut = slice(h * HD, (h + 1) * HD)
        put = slice(h * length, (h + 1) * length)
        qt[:, put] = q_ref[:, cut].T
        gt[:, put] = g_ref[:, cut].T

    pl.semaphore_wait(barrier, len(partners))

    def copy_col(k):
        part = kv.at[col, core, own]
        return pltpu.make_async_remote_copy(
            src_ref=part, dst_ref=part, send_sem=s1.at[k], recv_sem=r1.at[k],
            device_id=(row, later_col(k)), device_id_type=MESH,
        )

    def copy_chip(k, c):
        part = kv.at[earlier_col(k), core, own]
        return pltpu.make_async_remote_copy(
            src_ref=part, dst_ref=part, send_sem=s2.at[k, c], recv_sem=r2.at[k, c],
            device_id=(later_chip(c) * 2 + core, col), device_id_type=MESH,
        )

    def copy_core(k, c):
        part = kv.at[earlier_col(k), core, piece(earlier_chip(c))]
        return pltpu.make_async_remote_copy(
            src_ref=part, dst_ref=part, send_sem=s3.at[k, c], recv_sem=r3.at[k, c],
            device_id=(peer, col), device_id_type=MESH,
        )

    def copy_corner(k):
        turn = lax.rem(k, 2)
        source = (1 - turn) * far_x + turn * far_y
        target = (1 - turn) * far_y + turn * far_x
        part = kv.at[earlier_col(k), core, piece(source)]
        return pltpu.make_async_remote_copy(
            src_ref=part, dst_ref=part, send_sem=s2.at[k, 3], recv_sem=r2.at[k, 3],
            device_id=(target * 2 + core, col), device_id_type=MESH,
        )

    def send_chip(k, c):
        return copy_corner(k) if square and c == 3 else copy_chip(k, c)

    def spread(k):
        for c in range(1, 3 if square else chips):
            copy_chip(k, c).start()
        copy_core(k, 0).start()

    for k in range(1, cols_count):
        copy_col(k).start()
    spread(0)

    key_at = lax.broadcasted_iota(jnp.int32, (length, lanes), 0)
    row_at = lax.rem(lax.broadcasted_iota(jnp.int32, (length, lanes), 1), length)
    scores = jnp.where(key_at <= row_at, nn(k_ref[...], qt[...]), -BIG)
    first = jnp.max(scores, axis=0, keepdims=True)
    own_raised = jnp.exp2((scores - first) * SCALE)
    own_low = own_raised.astype(BF16)
    diag[...] = own_low
    top[...] = first
    tops[2 * cols_count * subs] = first
    total[...] = jnp.sum(own_raised, axis=0, keepdims=True)
    out_t[...] = tn(v_ref[...], own_low)

    def forward(key_col, which):
        @pl.loop(0, subs)
        def _(sub):
            at = pl.ds(pl.multiple_of(sub * tile, tile), tile)
            scores = nn(kv[key_col, which, at, 0:HD], qt[...])
            old = top[...]
            new = old
            offs = []
            for b in range(tile // length):
                block = ((sub * (tile // length) + b) * 2 + which) * cols_count + key_col
                off = jnp.where(order[block] < order[me], 0.0, BIG).astype(F32)
                offs.append(off)
                part = scores[b * length : (b + 1) * length]
                new = jnp.maximum(new, jnp.max(part, axis=0, keepdims=True) - off)
            alpha = jnp.exp2((old - new) * SCALE)
            shift = new * SCALE
            parts = []
            add = jnp.zeros_like(old)
            for b in range(tile // length):
                part = scores[b * length : (b + 1) * length]
                up = jnp.exp2(part * SCALE - (shift + offs[b]))
                add = add + jnp.sum(up, axis=0, keepdims=True)
                parts.append(up.astype(BF16))
            low = jnp.concatenate(parts, axis=0)
            index = (key_col * 2 + which) * subs + sub
            raised[index] = low
            top[...] = new
            tops[index] = new
            total[...] = total[...] * alpha + add
            out_t[...] = out_t[...] * alpha + tn(kv[key_col, which, at, HD : 2 * HD], low)

    @pl.loop(0, cols_count)
    def _(k):
        @pl.when(k < cols_count - 1)
        def _():
            copy_col(k + 1).wait_recv()
            spread(k + 1)

        if square:
            copy_chip(k, 1).wait_recv()
            copy_chip(k, 2).wait_recv()
            copy_corner(k).start()
            copy_core(k, 1).start()
            copy_core(k, 2).start()
            copy_corner(k).wait_recv()
            copy_core(k, 3).start()
        else:
            for c in range(1, chips):
                copy_chip(k, c).wait_recv()
                copy_core(k, c).start()
        forward(earlier_col(k), core)
        for c in range(chips):
            copy_core(k, c).wait_recv()
        forward(earlier_col(k), far)

    inverse = 1.0 / total[...]
    delta[...] = (
        jnp.sum(out_t[...] * gt[...].astype(F32), axis=0, keepdims=True) * inverse
    )

    def terms(values, keys, low, index):
        grad_weights = nn(values, gt[...])
        grad_low = (grad_weights - delta[...]).astype(BF16) * low
        share = jnp.exp2((tops[index] - top[...]) * SCALE) / total[...]
        scaled_q = (qt[...].astype(F32) * (share * ROOT)).astype(BF16)
        scaled_g = (gt[...].astype(F32) * share).astype(BF16)
        grad_q = tn(keys, grad_low) * (share * ROOT)
        return nt(grad_low, scaled_q), nt(low, scaled_g), grad_q

    dq_t[...] = jnp.zeros_like(dq_t)

    def backward(key_col, which, store):
        @pl.loop(0, subs)
        def _(sub):
            at = pl.ds(pl.multiple_of(sub * tile, tile), tile)
            index = (key_col * 2 + which) * subs + sub
            grad_k, grad_v, grad_q = terms(
                kv[key_col, which, at, HD : 2 * HD],
                kv[key_col, which, at, 0:HD],
                raised[index],
                index,
            )
            dq_t[...] += grad_q
            store(at, grad_k, grad_v)

    def give_core(k):
        return pltpu.make_async_remote_copy(
            src_ref=peer_send.at[k], dst_ref=peer_recv.at[k],
            send_sem=s4.at[k], recv_sem=r4.at[k],
            device_id=(peer, col), device_id_type=MESH,
        )

    def give_chip(k, c):
        return pltpu.make_async_remote_copy(
            src_ref=peer_recv.at[k, piece(later_chip(c))], dst_ref=chip_recv.at[k, c],
            send_sem=s5.at[k, c], recv_sem=r5.at[k, c],
            device_id=(later_chip(c) * 2 + core, col), device_id_type=MESH,
        )

    def give_col(k):
        return pltpu.make_async_remote_copy(
            src_ref=col_send.at[k], dst_ref=col_recv.at[k],
            send_sem=s6.at[k], recv_sem=r6.at[k],
            device_id=(row, later_col(k)), device_id_type=MESH,
        )

    def column_sum(k):
        result = keep[k]
        for c in range(1, chips):
            give_chip(k, c).wait_recv()
            result = result + chip_recv[k, c].astype(F32)
        return result

    def pass_on(k):
        col_send[k] = column_sum(k).astype(BF16)
        give_col(k).start()

    @pl.loop(0, cols_count)
    def _(step):
        k = lax.rem(step + 1, cols_count)

        def to_peer(at, grad_k, grad_v):
            peer_send[k, at, 0:HD] = grad_k.astype(BF16)
            peer_send[k, at, HD : 2 * HD] = grad_v.astype(BF16)

        backward(later_col(k), far, to_peer)
        give_core(k).start()

        def to_sum(at, grad_k, grad_v):
            chip_sum[at, 0:HD] = grad_k
            chip_sum[at, HD : 2 * HD] = grad_v

        backward(later_col(k), core, to_sum)
        give_core(k).wait_recv()
        keep[k] = chip_sum[own] + peer_recv[k, own].astype(F32)
        peer_recv[k] = (chip_sum[...] + peer_recv[k].astype(F32)).astype(BF16)
        for c in range(1, chips):
            give_chip(k, c).start()

        @pl.when(step > 1)
        def _():
            pass_on(step - 1)

    own_dk, own_dv, own_dq = terms(
        v_ref[...], k_ref[...], diag[...], 2 * cols_count * subs
    )
    own_sum[:, 0:HD] = own_dk
    own_sum[:, HD : 2 * HD] = own_dv
    dq_t[...] += own_dq
    for k in range(max(1, cols_count - 1), cols_count):
        pass_on(k)
    for h in range(heads):
        cut = slice(h * HD, (h + 1) * HD)
        put = slice(h * length, (h + 1) * length)
        dq_ref[:, cut] = dq_t[:, put].T.astype(BF16)
    last = own_sum[...] + column_sum(0)
    for k in range(1, cols_count):
        give_col(k).wait_recv()
        last = last + col_recv[k].astype(F32)
    dk_ref[...] = last[:, 0:HD].astype(BF16)
    dv_ref[...] = last[:, HD : 2 * HD].astype(BF16)

    for k in range(1, cols_count):
        copy_col(k).wait_send()
        give_col(k).wait_send()
    for k in range(cols_count):
        give_core(k).wait_send()
        copy_core(k, 0).wait_send()
        for c in range(1, chips):
            send_chip(k, c).wait_send()
            copy_core(k, c).wait_send()
            give_chip(k, c).wait_send()


def per_device(queries, keys, values, grad_out, block_order):
    rows_count = lax.axis_size("qrow")
    cols_count = lax.axis_size("kcol")
    length = queries.shape[0]
    heads = queries.shape[1] // HD
    chips = rows_count // 2
    span = chips * length
    tile = min(512, span)
    subs = span // tile
    lanes = heads * length
    vmem = pl.BlockSpec(memory_space=pltpu.VMEM)
    dma = pltpu.SemaphoreType.DMA
    return pl.pallas_call(
        functools.partial(kernel, rows_count, cols_count, length, heads, tile),
        out_shape=(
            jax.ShapeDtypeStruct(queries.shape, BF16),
            jax.ShapeDtypeStruct(keys.shape, BF16),
            jax.ShapeDtypeStruct(values.shape, BF16),
        ),
        in_specs=[pl.BlockSpec(memory_space=pltpu.SMEM)] + [vmem] * 4,
        out_specs=(vmem, vmem, vmem),
        scratch_shapes=[
            pltpu.VMEM((cols_count, 2, span, 2 * HD), BF16),
            pltpu.VMEM((2 * cols_count * subs, tile, lanes), BF16),
            pltpu.VMEM((HD, lanes), BF16),
            pltpu.VMEM((HD, lanes), BF16),
            pltpu.VMEM((2 * cols_count * subs + 1, 1, lanes), F32),
            pltpu.VMEM((1, lanes), F32),
            pltpu.VMEM((1, lanes), F32),
            pltpu.VMEM((HD, lanes), F32),
            pltpu.VMEM((1, lanes), F32),
            pltpu.VMEM((HD, lanes), F32),
            pltpu.VMEM((length, lanes), BF16),
            pltpu.VMEM((length, 2 * HD), F32),
            pltpu.VMEM((span, 2 * HD), F32),
            pltpu.VMEM((cols_count, length, 2 * HD), F32),
            pltpu.VMEM((cols_count, span, 2 * HD), BF16),
            pltpu.VMEM((cols_count, span, 2 * HD), BF16),
            pltpu.VMEM((cols_count, chips, length, 2 * HD), BF16),
            pltpu.VMEM((cols_count, length, 2 * HD), BF16),
            pltpu.VMEM((cols_count, length, 2 * HD), BF16),
            dma((cols_count,)), dma((cols_count,)),
            dma((cols_count, chips)), dma((cols_count, chips)),
            dma((cols_count, chips)), dma((cols_count, chips)),
            dma((cols_count,)), dma((cols_count,)),
            dma((cols_count, chips)), dma((cols_count, chips)),
            dma((cols_count,)), dma((cols_count,)),
        ],
        compiler_params=pltpu.CompilerParams(
            collective_id=0, has_side_effects=True, vmem_limit_bytes=62 * 1024 * 1024
        ),
    )(block_order, queries, keys, values, grad_out)


def solution(mesh):
    return jax.shard_map(
        per_device,
        mesh=mesh,
        in_specs=(
            P(("qrow", "kcol"), None),
            P(("qrow", "kcol"), None),
            P(("qrow", "kcol"), None),
            P(("qrow", "kcol"), None),
            P(),
        ),
        out_specs=(P(("qrow", "kcol"), None), P(("qrow", "kcol"), None), P(("qrow", "kcol"), None)),
        check_vma=False,
    )
```

```python
import functools
import math

import jax
import jax.numpy as jnp
from jax import lax
from jax.experimental import pallas as pl
from jax.experimental.pallas import tpu as pltpu
from jax.sharding import PartitionSpec as P

HD = 128
BIG = 1e30
F32 = jnp.float32
BF16 = jnp.bfloat16
ROOT = 1.0 / math.sqrt(HD)
SCALE = ROOT / math.log(2.0)
MESH = pl.DeviceIdType.MESH


def nn(a, b):
    return lax.dot_general(a, b, (((1,), (0,)), ((), ())), preferred_element_type=F32)


def nt(a, b):
    return lax.dot_general(a, b, (((1,), (1,)), ((), ())), preferred_element_type=F32)


def tn(a, b):
    return lax.dot_general(a, b, (((0,), (0,)), ((), ())), preferred_element_type=F32)


def kernel(
    rows_count, cols_count, length, heads, tile,
    order, q_ref, k_ref, v_ref, g_ref, dq_ref, dk_ref, dv_ref,
    kv, raised, qt, gt, tops, top, total, out_t, delta, dq_t, diag,
    own_sum, chip_sum, keep, peer_send, peer_recv, chip_recv, col_send, col_recv,
    s1, r1, s2, r2, s3, r3, s4, r4, s5, r5, s6, r6,
):
    chips = rows_count // 2
    row = lax.axis_index("qrow")
    col = lax.axis_index("kcol")
    chip = lax.div(row, 2)
    core = lax.rem(row, 2)
    far = 1 - core
    peer = chip * 2 + far
    me = row * cols_count + col
    span = chips * length
    subs = span // tile
    lanes = heads * length

    def later_col(k):
        return lax.rem(col + k, cols_count)

    def earlier_col(k):
        return lax.rem(col + cols_count - k, cols_count)

    def later_chip(c):
        return lax.rem(chip + c, chips)

    def earlier_chip(c):
        return lax.rem(chip + chips - c, chips)

    def piece(c):
        return pl.ds(pl.multiple_of(c * length, length), length)

    barrier = pltpu.get_barrier_semaphore()
    partners = [(row, later_col(k)) for k in range(1, cols_count)]
    partners += [(later_chip(c) * 2 + core, col) for c in range(1, chips)]
    partners += [(peer, col)]
    for partner in partners:
        pl.semaphore_signal(barrier, inc=1, device_id=partner, device_id_type=MESH)
    own = piece(chip)
    kv[col, core, own, 0:HD] = k_ref[...]
    kv[col, core, own, HD : 2 * HD] = v_ref[...]

    for h in range(heads):
        cut = slice(h * HD, (h + 1) * HD)
        put = slice(h * length, (h + 1) * length)
        qt[:, put] = q_ref[:, cut].T
        gt[:, put] = g_ref[:, cut].T

    pl.semaphore_wait(barrier, len(partners))

    def copy_col(k):
        part = kv.at[col, core, own]
        return pltpu.make_async_remote_copy(
            src_ref=part, dst_ref=part, send_sem=s1.at[k], recv_sem=r1.at[k],
            device_id=(row, later_col(k)), device_id_type=MESH,
        )

    def copy_chip(k, c):
        part = kv.at[earlier_col(k), core, own]
        return pltpu.make_async_remote_copy(
            src_ref=part, dst_ref=part, send_sem=s2.at[k, c], recv_sem=r2.at[k, c],
            device_id=(later_chip(c) * 2 + core, col), device_id_type=MESH,
        )

    def copy_core(k, c):
        part = kv.at[earlier_col(k), core, piece(earlier_chip(c))]
        return pltpu.make_async_remote_copy(
            src_ref=part, dst_ref=part, send_sem=s3.at[k, c], recv_sem=r3.at[k, c],
            device_id=(peer, col), device_id_type=MESH,
        )

    def spread(k):
        for c in range(1, chips):
            copy_chip(k, c).start()
        copy_core(k, 0).start()

    for k in range(1, cols_count):
        copy_col(k).start()
    spread(0)

    key_at = lax.broadcasted_iota(jnp.int32, (length, lanes), 0)
    row_at = lax.rem(lax.broadcasted_iota(jnp.int32, (length, lanes), 1), length)
    scores = jnp.where(key_at <= row_at, nn(k_ref[...], qt[...]), -BIG)
    first = jnp.max(scores, axis=0, keepdims=True)
    own_raised = jnp.exp2((scores - first) * SCALE)
    own_low = own_raised.astype(BF16)
    diag[...] = own_low
    top[...] = first
    tops[2 * cols_count * subs] = first
    total[...] = jnp.sum(own_raised, axis=0, keepdims=True)
    out_t[...] = tn(v_ref[...], own_low)

    def forward(key_col, which):
        @pl.loop(0, subs)
        def _(sub):
            at = pl.ds(pl.multiple_of(sub * tile, tile), tile)
            scores = nn(kv[key_col, which, at, 0:HD], qt[...])
            old = top[...]
            new = old
            offs = []
            for b in range(tile // length):
                block = ((sub * (tile // length) + b) * 2 + which) * cols_count + key_col
                off = jnp.where(order[block] < order[me], 0.0, BIG).astype(F32)
                offs.append(off)
                part = scores[b * length : (b + 1) * length]
                new = jnp.maximum(new, jnp.max(part, axis=0, keepdims=True) - off)
            alpha = jnp.exp2((old - new) * SCALE)
            shift = new * SCALE
            parts = []
            add = jnp.zeros_like(old)
            for b in range(tile // length):
                part = scores[b * length : (b + 1) * length]
                up = jnp.exp2(part * SCALE - (shift + offs[b]))
                add = add + jnp.sum(up, axis=0, keepdims=True)
                parts.append(up.astype(BF16))
            low = jnp.concatenate(parts, axis=0)
            index = (key_col * 2 + which) * subs + sub
            raised[index] = low
            top[...] = new
            tops[index] = new
            total[...] = total[...] * alpha + add
            out_t[...] = out_t[...] * alpha + tn(kv[key_col, which, at, HD : 2 * HD], low)

    @pl.loop(1, cols_count)
    def _(k):
        copy_col(k).wait_recv()
        spread(k)

    @pl.loop(0, cols_count)
    def _(k):
        for c in range(1, chips):
            copy_chip(k, c).wait_recv()
            copy_core(k, c).start()
        forward(earlier_col(k), core)
        for c in range(chips):
            copy_core(k, c).wait_recv()
        forward(earlier_col(k), far)

    inverse = 1.0 / total[...]
    delta[...] = (
        jnp.sum(out_t[...] * gt[...].astype(F32), axis=0, keepdims=True) * inverse
    )

    def terms(values, keys, low, index):
        grad_weights = nn(values, gt[...])
        grad_low = (grad_weights - delta[...]).astype(BF16) * low
        share = jnp.exp2((tops[index] - top[...]) * SCALE) / total[...]
        scaled_q = (qt[...].astype(F32) * (share * ROOT)).astype(BF16)
        scaled_g = (gt[...].astype(F32) * share).astype(BF16)
        grad_q = tn(keys, grad_low) * (share * ROOT)
        return nt(grad_low, scaled_q), nt(low, scaled_g), grad_q

    dq_t[...] = jnp.zeros_like(dq_t)

    def backward(key_col, which, store):
        @pl.loop(0, subs)
        def _(sub):
            at = pl.ds(pl.multiple_of(sub * tile, tile), tile)
            index = (key_col * 2 + which) * subs + sub
            grad_k, grad_v, grad_q = terms(
                kv[key_col, which, at, HD : 2 * HD],
                kv[key_col, which, at, 0:HD],
                raised[index],
                index,
            )
            dq_t[...] += grad_q
            store(at, grad_k, grad_v)

    def give_core(k):
        return pltpu.make_async_remote_copy(
            src_ref=peer_send.at[k], dst_ref=peer_recv.at[k],
            send_sem=s4.at[k], recv_sem=r4.at[k],
            device_id=(peer, col), device_id_type=MESH,
        )

    def give_chip(k, c):
        return pltpu.make_async_remote_copy(
            src_ref=peer_recv.at[k, piece(later_chip(c))], dst_ref=chip_recv.at[k, c],
            send_sem=s5.at[k, c], recv_sem=r5.at[k, c],
            device_id=(later_chip(c) * 2 + core, col), device_id_type=MESH,
        )

    def give_col(k):
        return pltpu.make_async_remote_copy(
            src_ref=col_send.at[k], dst_ref=col_recv.at[k],
            send_sem=s6.at[k], recv_sem=r6.at[k],
            device_id=(row, later_col(k)), device_id_type=MESH,
        )

    def column_sum(k):
        result = keep[k]
        for c in range(1, chips):
            give_chip(k, c).wait_recv()
            result = result + chip_recv[k, c].astype(F32)
        return result

    def pass_on(k):
        col_send[k] = column_sum(k).astype(BF16)
        give_col(k).start()

    @pl.loop(0, cols_count)
    def _(step):
        k = lax.rem(step + 1, cols_count)

        def to_peer(at, grad_k, grad_v):
            peer_send[k, at, 0:HD] = grad_k.astype(BF16)
            peer_send[k, at, HD : 2 * HD] = grad_v.astype(BF16)

        backward(later_col(k), far, to_peer)
        give_core(k).start()

        def to_sum(at, grad_k, grad_v):
            chip_sum[at, 0:HD] = grad_k
            chip_sum[at, HD : 2 * HD] = grad_v

        backward(later_col(k), core, to_sum)
        give_core(k).wait_recv()
        keep[k] = chip_sum[own] + peer_recv[k, own].astype(F32)
        peer_recv[k] = (chip_sum[...] + peer_recv[k].astype(F32)).astype(BF16)
        for c in range(1, chips):
            give_chip(k, c).start()

        @pl.when(step > 1)
        def _():
            pass_on(step - 1)

    own_dk, own_dv, own_dq = terms(
        v_ref[...], k_ref[...], diag[...], 2 * cols_count * subs
    )
    own_sum[:, 0:HD] = own_dk
    own_sum[:, HD : 2 * HD] = own_dv
    dq_t[...] += own_dq
    for k in range(max(1, cols_count - 1), cols_count):
        pass_on(k)
    for h in range(heads):
        cut = slice(h * HD, (h + 1) * HD)
        put = slice(h * length, (h + 1) * length)
        dq_ref[:, cut] = dq_t[:, put].T.astype(BF16)
    last = own_sum[...] + column_sum(0)
    for k in range(1, cols_count):
        give_col(k).wait_recv()
        last = last + col_recv[k].astype(F32)
    dk_ref[...] = last[:, 0:HD].astype(BF16)
    dv_ref[...] = last[:, HD : 2 * HD].astype(BF16)

    for k in range(1, cols_count):
        copy_col(k).wait_send()
        give_col(k).wait_send()
    for k in range(cols_count):
        give_core(k).wait_send()
        copy_core(k, 0).wait_send()
        for c in range(1, chips):
            copy_chip(k, c).wait_send()
            copy_core(k, c).wait_send()
            give_chip(k, c).wait_send()


def per_device(queries, keys, values, grad_out, block_order):
    rows_count = lax.axis_size("qrow")
    cols_count = lax.axis_size("kcol")
    length = queries.shape[0]
    heads = queries.shape[1] // HD
    chips = rows_count // 2
    span = chips * length
    tile = min(512, span)
    subs = span // tile
    lanes = heads * length
    vmem = pl.BlockSpec(memory_space=pltpu.VMEM)
    dma = pltpu.SemaphoreType.DMA
    return pl.pallas_call(
        functools.partial(kernel, rows_count, cols_count, length, heads, tile),
        out_shape=(
            jax.ShapeDtypeStruct(queries.shape, BF16),
            jax.ShapeDtypeStruct(keys.shape, BF16),
            jax.ShapeDtypeStruct(values.shape, BF16),
        ),
        in_specs=[pl.BlockSpec(memory_space=pltpu.SMEM)] + [vmem] * 4,
        out_specs=(vmem, vmem, vmem),
        scratch_shapes=[
            pltpu.VMEM((cols_count, 2, span, 2 * HD), BF16),
            pltpu.VMEM((2 * cols_count * subs, tile, lanes), BF16),
            pltpu.VMEM((HD, lanes), BF16),
            pltpu.VMEM((HD, lanes), BF16),
            pltpu.VMEM((2 * cols_count * subs + 1, 1, lanes), F32),
            pltpu.VMEM((1, lanes), F32),
            pltpu.VMEM((1, lanes), F32),
            pltpu.VMEM((HD, lanes), F32),
            pltpu.VMEM((1, lanes), F32),
            pltpu.VMEM((HD, lanes), F32),
            pltpu.VMEM((length, lanes), BF16),
            pltpu.VMEM((length, 2 * HD), F32),
            pltpu.VMEM((span, 2 * HD), F32),
            pltpu.VMEM((cols_count, length, 2 * HD), F32),
            pltpu.VMEM((cols_count, span, 2 * HD), BF16),
            pltpu.VMEM((cols_count, span, 2 * HD), BF16),
            pltpu.VMEM((cols_count, chips, length, 2 * HD), BF16),
            pltpu.VMEM((cols_count, length, 2 * HD), BF16),
            pltpu.VMEM((cols_count, length, 2 * HD), BF16),
            dma((cols_count,)), dma((cols_count,)),
            dma((cols_count, chips)), dma((cols_count, chips)),
            dma((cols_count, chips)), dma((cols_count, chips)),
            dma((cols_count,)), dma((cols_count,)),
            dma((cols_count, chips)), dma((cols_count, chips)),
            dma((cols_count,)), dma((cols_count,)),
        ],
        compiler_params=pltpu.CompilerParams(
            collective_id=0, has_side_effects=True, vmem_limit_bytes=62 * 1024 * 1024
        ),
    )(block_order, queries, keys, values, grad_out)


def solution(mesh):
    return jax.shard_map(
        per_device,
        mesh=mesh,
        in_specs=(
            P(("qrow", "kcol"), None),
            P(("qrow", "kcol"), None),
            P(("qrow", "kcol"), None),
            P(("qrow", "kcol"), None),
            P(),
        ),
        out_specs=(P(("qrow", "kcol"), None), P(("qrow", "kcol"), None), P(("qrow", "kcol"), None)),
        check_vma=False,
    )
```
